32 devices in a mesh: tp: 16 (over z, y, core), dp: 2 (over x).
Axes of the slice: x: 2, y: 2, z: 4, core: 2. Of those that a mesh axis runs over, the one named last changes fastest.
Arguments:
- tokens: bfloat16 [512, 8192], P('dp', 'tp'), parts along dimension 0, may hold values from -6 to 6
- grad_out: bfloat16 [512, 8192], P('dp', 'tp'), parts along dimension 0, may hold values from -6 to 6
- gate_blocks: bfloat16 [8192, 128, 128], P('tp'), may hold values from -0.09375 to 0.09375
- gate_index: int32 [128, 64], P('tp'), may hold values from 0 to 63, as said below
- gate_count: int32 [128], P('tp'), may hold values from 16 to 64, as said below
- up_blocks: bfloat16 [8192, 128, 128], P('tp'), may hold values from -0.09375 to 0.09375
- up_index: int32 [128, 64], P('tp'), may hold values from 0 to 63, as said below
- up_count: int32 [128], P('tp'), may hold values from 16 to 64, as said below
- down_blocks: bfloat16 [8192, 128, 128], P('tp'), may hold values from -0.0625 to 0.0625
- down_index: int32 [128, 64], P('tp'), may hold values from 0 to 63, as said below
- down_count: int32 [128], P('tp'), may hold values from 16 to 64, as said below
Outputs:
- outputs: bfloat16 [512, 8192], P('dp', 'tp'), parts along dimension 0
- grad_tokens: bfloat16 [512, 8192], P('dp', 'tp'), parts along dimension 0
The draws below stay inside these ranges and needn't reach their ends.
There are 2 independent parts, one for each index of `dp`. The reference program is written for one: setup_inputs(seed, part) draws one part's arguments, and reference() takes and returns one part's arrays. A program takes and returns all parts, laid end to end along the dimension named above; an argument that names none is the same for every part. Nothing has to cross between parts.
Inputs may be any that keep to these rules, and one draw needn't show every extreme that they name: `gate_index`: each row is an ordering of the 64 block rows; entries at positions from gate_count onward are ignored. `gate_count`: both ends occur. `up_index`: each row is an ordering of the 64 block rows; entries at positions from up_count onward are ignored. `up_count`: both ends occur. `down_index`: each row is an ordering of the 64 block columns; entries at positions from down_count onward are ignored. `down_count`: both ends occur.
All inputs are finite; a program needn't handle non-finite values.
Results may differ from the reference program's by a relative error of at most 0.005.
Values may be sent and summed in bfloat16 or wider, within the bound.
A program may use at most 192 MiB of HBM per device.

```python
import jax
import jax.numpy as jnp

D = 8192
FF = 16384
BLK = 128
TOKENS = 256
SLOTS = 64
HBLK = 128


def layout(key, marker):
    base = jax.random.fold_in(key, marker)
    first, second, third = jax.random.split(base, 3)
    counts = jax.random.randint(first, (HBLK,), SLOTS // 4, 3 * SLOTS // 4 + 1)
    order = jax.random.permutation(second, HBLK)
    counts = counts.at[order[0]].set(SLOTS).at[order[1]].set(SLOTS // 4)
    orders = jax.vmap(lambda single: jax.random.permutation(single, SLOTS))(jax.random.split(third, HBLK))
    return (orders.astype(jnp.int32), counts.astype(jnp.int32))


def draw_gate_index(key, part):
    return layout(key, 11)[0]


def draw_gate_count(key, part):
    return layout(key, 11)[1]


def draw_up_index(key, part):
    return layout(key, 12)[0]


def draw_up_count(key, part):
    return layout(key, 12)[1]


def draw_down_index(key, part):
    return layout(key, 13)[0]


def draw_down_count(key, part):
    return layout(key, 13)[1]


def block_scale(stream_key, shape, shards, least, high):
    def one(dim, shards_of):
        heights = jax.random.uniform(jax.random.fold_in(jax.random.fold_in(stream_key, 6), dim), (shards_of,), jnp.float32, least / len(shards), high / len(shards))
        return jnp.repeat(jnp.exp(heights), shape[dim] // shards_of).reshape((-1,) + (1,) * (len(shape) - dim - 1))

    level = one(*shards[0])
    for cut in shards[1:]:
        level = level * one(*cut)
    return level


def normal_values(key, extent, spread, limit, cuts=(), held_as=jnp.bfloat16):
    gain = block_scale(key, extent, cuts, -0.22, 0.18) if cuts else 1.0
    drawn = jax.random.normal(key, extent, jnp.float32) * spread * gain
    return jnp.minimum(jnp.maximum(drawn, -limit), limit).astype(held_as)


def setup_inputs(seed: int = 0, part: int = 0) -> dict:
    seeds = jax.random.split(jax.random.key(seed), 12)
    part_keys = jax.random.split(jax.random.fold_in(seeds[11], part), 12)
    return {
        "tokens": normal_values(part_keys[0], (TOKENS, D), 1.0, 6.0, ((1, 16),)),
        "grad_out": normal_values(part_keys[1], (TOKENS, D), 1.0, 6.0, ((1, 16),)),
        "gate_blocks": normal_values(seeds[2], (HBLK * SLOTS, BLK, BLK), (D // 2) ** -0.5, 0.09375, ((0, 16),)),
        "gate_index": draw_gate_index(jax.random.fold_in(seeds[11], 71), part),
        "gate_count": draw_gate_count(jax.random.fold_in(seeds[11], 71), part),
        "up_blocks": normal_values(seeds[5], (HBLK * SLOTS, BLK, BLK), (D // 2) ** -0.5, 0.09375, ((0, 16),)),
        "up_index": draw_up_index(jax.random.fold_in(seeds[11], 71), part),
        "up_count": draw_up_count(jax.random.fold_in(seeds[11], 71), part),
        "down_blocks": normal_values(seeds[8], (HBLK * SLOTS, BLK, BLK), (FF // 2) ** -0.5, 0.0625, ((0, 16),)),
        "down_index": draw_down_index(jax.random.fold_in(seeds[11], 71), part),
        "down_count": draw_down_count(jax.random.fold_in(seeds[11], 71), part),
    }


def expand(blocks, index, count):
    live = jnp.arange(SLOTS, dtype=jnp.int32)[None, :] < count[:, None]
    kept = jnp.where(live[:, :, None, None], blocks.reshape(HBLK, SLOTS, BLK, BLK), jnp.zeros((), blocks.dtype))
    owners = jnp.broadcast_to(jnp.arange(HBLK, dtype=jnp.int32)[:, None], (HBLK, SLOTS))
    return jnp.zeros_like(kept).at[owners, index.astype(jnp.int32)].set(kept)


def column_matrix(blocks, index, count):
    return expand(blocks, index, count).transpose(1, 2, 0, 3).reshape(D, FF)


def reference(tokens, grad_out, gate_blocks, gate_index, gate_count, up_blocks, up_index, up_count, down_blocks, down_index, down_count):
    gate_weight = column_matrix(gate_blocks, gate_index, gate_count)
    up_weight = column_matrix(up_blocks, up_index, up_count)
    down_weight = expand(down_blocks, down_index, down_count).transpose(0, 2, 1, 3).reshape(FF, D)
    gate = jnp.dot(tokens, gate_weight, preferred_element_type=jnp.float32)
    upper = jnp.dot(tokens, up_weight, preferred_element_type=jnp.float32)
    sigma = jax.nn.sigmoid(gate)
    hidden = (gate * sigma * upper).astype(jnp.bfloat16)
    outputs = jnp.dot(hidden, down_weight, preferred_element_type=jnp.float32).astype(jnp.bfloat16)
    grad_hidden = jnp.dot(grad_out, down_weight.T, preferred_element_type=jnp.float32)
    grad_gate = (grad_hidden * upper * sigma * (1.0 + gate * (1.0 - sigma))).astype(jnp.bfloat16)
    grad_up = (grad_hidden * gate * sigma).astype(jnp.bfloat16)
    total = jnp.dot(grad_gate, gate_weight.T, preferred_element_type=jnp.float32) + jnp.dot(grad_up, up_weight.T, preferred_element_type=jnp.float32)
    return outputs, total.astype(jnp.bfloat16)
```

```python
import functools

import jax
import jax.numpy as jnp
from jax import lax
from jax.experimental import pallas as pl
from jax.experimental.pallas import tpu as pltpu
from jax.sharding import PartitionSpec as P


MESH = pl.DeviceIdType.MESH
CORES = 2
ROWS = 2
VMEM_LIMIT = 60 * 1024 * 1024


def places(index, count):
    hidden_blocks, slots = index.shape
    slot = lax.broadcasted_iota(jnp.int32, (hidden_blocks, slots, slots), 1)
    place = lax.broadcasted_iota(jnp.int32, (hidden_blocks, slots, slots), 2)
    where = jnp.sum(jnp.where(index[:, :, None] == place, slot, 0), axis=1)
    base = lax.broadcasted_iota(jnp.int32, (hidden_blocks, slots), 0) * slots
    return jnp.where(where < count[:, None], base + where, hidden_blocks * slots)


def position(depth):
    me = lax.axis_index("tp")
    core = lax.rem(me, CORES)
    row = lax.rem(me // CORES, ROWS)
    layer = me // (CORES * ROWS)
    return me, layer, row, core


def shard_of(layer, row, core):
    return (layer * ROWS + row) * CORES + core


def greet(depth):
    me, layer, row, core = position(depth)
    barrier = pltpu.get_barrier_semaphore()
    partners = [shard_of(layer, row, 1 - core), shard_of(layer, 1 - row, core)]
    partners += [shard_of(lax.rem(layer + k, depth), row, core) for k in range(1, depth)]
    for partner in partners:
        pl.semaphore_signal(barrier, inc=1, device_id={"tp": partner}, device_id_type=MESH)
    pl.semaphore_wait(barrier, len(partners))


def remote(src, dst, send, recv, target):
    return pltpu.make_async_remote_copy(
        src_ref=src,
        dst_ref=dst,
        send_sem=send,
        recv_sem=recv,
        device_id={"tp": target},
        device_id_type=MESH,
    )


def load_copies(hbm, buffer, sems, hidden_blocks, slots):
    return [
        pltpu.make_async_copy(
            hbm.at[pl.ds(h * slots, slots)], buffer.at[pl.ds(h * slots, slots)], sems.at[h]
        )
        for h in range(hidden_blocks)
    ]


class Gather:
    def __init__(self, depth, full, sems):
        self.depth, self.full = depth, full
        self.z_send, self.z_recv, self.y_send, self.y_recv, self.c_send, self.c_recv = sems
        self.me, self.layer, self.row, self.core = position(depth)

    def back(self, k):
        return lax.rem(self.layer - k + self.depth, self.depth)

    def z(self, k, shard):
        target = shard_of(lax.rem(self.layer + k, self.depth), self.row, self.core)
        block = self.full.at[shard]
        return remote(block, block, self.z_send.at[k], self.z_recv.at[k], target)

    def y(self, k, shard):
        block = self.full.at[shard]
        target = shard_of(self.layer, 1 - self.row, self.core)
        return remote(block, block, self.y_send.at[k], self.y_recv.at[k], target)

    def c(self, k, shard):
        block = self.full.at[shard]
        target = shard_of(self.layer, self.row, 1 - self.core)
        return remote(block, block, self.c_send.at[k], self.c_recv.at[k], target)

    def start_layers(self):
        for k in range(1, self.depth):
            self.z(k, self.me).start()

    def start_own(self):
        self.y(0, self.me).start()
        self.c(0, self.me).start()

    def from_layer(self, k):
        shard = shard_of(self.back(k), self.row, self.core)
        self.z(k, shard).wait_recv()
        self.y(k, shard).start()
        self.c(k, shard).start()

    def from_row(self, k):
        shard = shard_of(self.back(k), 1 - self.row, self.core)
        self.y(k, shard).wait_recv()
        self.c(self.depth + k, shard).start()

    def chip_own(self, k):
        self.c(k, shard_of(self.back(k), self.row, 1 - self.core)).wait_recv()
        return self.back(k) * ROWS + self.row

    def chip_other(self, k):
        self.c(self.depth + k, shard_of(self.back(k), 1 - self.row, 1 - self.core)).wait_recv()
        return self.back(k) * ROWS + 1 - self.row

    def finish(self):
        for k in range(1, self.depth):
            self.z(k, self.me).wait_send()
        for k in range(self.depth):
            self.y(k, self.me).wait_send()
        for k in range(2 * self.depth):
            self.c(k, self.me).wait_send()


def each(low, high, step):
    def run(k, carry):
        step(k)
        return carry

    lax.fori_loop(low, high, run, 0)


def dot(left, right, contract=0):
    return lax.dot_general(
        left, right, (((1,), (contract,)), ((), ())), preferred_element_type=jnp.float32
    )


def first_kernel(depth, hidden_blocks, slots, block, *refs):
    (tokens, grads, at_gate, at_up, at_down, gate_hbm, up_hbm, down_hbm) = refs[:8]
    (hidden, grad_gate, grad_up) = refs[8:11]
    (first, second, all_tokens, all_grads, projected, grad_hidden, load_sems) = refs[11:18]
    token_sems, grad_sems = refs[18:24], refs[24:30]
    me = position(depth)[0]
    per_chip = slots // (depth * ROWS)
    loads = load_copies(gate_hbm, first, load_sems.at[0], hidden_blocks, slots)
    loads += load_copies(up_hbm, second, load_sems.at[1], hidden_blocks, slots)
    down_loads = load_copies(down_hbm, first, load_sems.at[2], hidden_blocks, slots)
    for load in loads:
        load.start()
    all_tokens[me] = tokens[...]
    all_grads[me] = grads[...]
    greet(depth)
    tok = Gather(depth, all_tokens, token_sems)
    grd = Gather(depth, all_grads, grad_sems)
    tok.start_layers()
    tok.start_own()
    grd.start_own()
    first[hidden_blocks * slots] = jnp.zeros((block, block), first.dtype)
    second[hidden_blocks * slots] = jnp.zeros((block, block), second.dtype)
    projected[...] = jnp.zeros_like(projected)
    grad_hidden[...] = jnp.zeros_like(grad_hidden)
    for load in loads:
        load.wait()

    def pair(full, chip):
        return jnp.concatenate([full[CORES * chip + i] for i in range(CORES)], axis=1)

    def project(chip):
        def one(h):
            rows = [
                jnp.concatenate(
                    [first[at_gate[h, chip * per_chip + j]], second[at_up[h, chip * per_chip + j]]], axis=1
                )
                for j in range(per_chip)
            ]
            projected[h] += dot(pair(all_tokens, chip), jnp.concatenate(rows, axis=0))

        each(0, hidden_blocks, one)

    def push_back(chip):
        def one(p):
            rows = [
                jnp.concatenate(
                    [first[at_down[2 * p + i, chip * per_chip + j]] for j in range(per_chip)], axis=1
                )
                for i in range(2)
            ]
            grad_hidden[p] += dot(pair(all_grads, chip), jnp.concatenate(rows, axis=0), 1)

        each(0, hidden_blocks // 2, one)

    def run(gather, work, between):
        def layer_step(k):
            gather.from_layer(k)
            gather.from_row(k - 1)
            work(gather.chip_own(k - 1))

        each(1, depth, layer_step)
        between()
        gather.from_row(depth - 1)
        work(gather.chip_own(depth - 1))
        each(0, depth, lambda k: work(gather.chip_other(k)))

    run(tok, project, grd.start_layers)
    for load in down_loads:
        load.start()

    def activate(h):
        gate, up = projected[h][:, :block], projected[h][:, block:]
        hidden[h] = (gate * jax.nn.sigmoid(gate) * up).astype(hidden.dtype)

    each(0, hidden_blocks, activate)
    for load in down_loads:
        load.wait()
    run(grd, push_back, lambda: None)

    def back(p):
        for i in range(2):
            h = 2 * p + i
            gate, up = projected[h][:, :block], projected[h][:, block:]
            flow = grad_hidden[p][:, i * block : (i + 1) * block]
            sigma = jax.nn.sigmoid(gate)
            grad_gate[h] = (flow * up * sigma * (1.0 + gate * (1.0 - sigma))).astype(grad_gate.dtype)
            grad_up[h] = (flow * gate * sigma).astype(grad_up.dtype)

    each(0, hidden_blocks // 2, back)
    tok.finish()
    grd.finish()


class Scatter:
    def __init__(self, depth, partial, held, bufs):
        self.depth, self.partial, self.held = depth, partial, held
        (self.c_out, self.c_in, self.y_out, self.y_in, self.z_out, self.z_in) = bufs[:6]
        (self.c_send, self.c_recv, self.y_send, self.y_recv, self.z_send, self.z_recv) = bufs[6:]
        self.me, self.layer, self.row, self.core = position(depth)

    def ahead(self, k):
        return lax.rem(self.layer + k, self.depth)

    def c(self, i):
        target = shard_of(self.layer, self.row, 1 - self.core)
        return remote(self.c_out.at[i], self.c_in.at[i], self.c_send.at[i], self.c_recv.at[i], target)

    def y(self, k):
        target = shard_of(self.layer, 1 - self.row, self.core)
        return remote(self.y_out.at[k], self.y_in.at[k], self.y_send.at[k], self.y_recv.at[k], target)

    def z(self, k):
        target = shard_of(self.ahead(k), self.row, self.core)
        return remote(self.z_out.at[k], self.z_in.at[k], self.z_send.at[k], self.z_recv.at[k], target)

    def sibling(self, k, other):
        row = 1 - self.row if other else self.row
        i = k if other else self.depth + k
        for cols, value in self.partial(shard_of(self.ahead(k), row, 1 - self.core)):
            self.c_out[i, :, cols] = value.astype(self.c_out.dtype)
        self.c(i).start()

    def across(self, k):
        parts = self.partial(shard_of(self.ahead(k), 1 - self.row, self.core))
        self.c(k).wait_recv()
        for cols, value in parts:
            total = value + self.c_in[k, :, cols].astype(jnp.float32)
            self.y_out[k, :, cols] = total.astype(self.y_out.dtype)
        self.y(k).start()

    def keep(self, k):
        parts = self.partial(shard_of(self.ahead(k), self.row, self.core))
        self.c(self.depth + k).wait_recv()
        for cols, value in parts:
            self.held[k, :, cols] = value + self.c_in[self.depth + k, :, cols].astype(jnp.float32)

    def along(self, k):
        self.y(k).wait_recv()
        total = self.held[k] + self.y_in[k].astype(jnp.float32)
        self.z_out[k] = total.astype(self.z_out.dtype)
        self.z(k).start()

    def result(self, out):
        self.y(0).wait_recv()
        total = self.held[0] + self.y_in[0].astype(jnp.float32)
        for k in range(1, self.depth):
            self.z(k).wait_recv()
            total = total + self.z_in[k].astype(jnp.float32)
        out[...] = total.astype(out.dtype)

    def finish(self):
        for i in range(2 * self.depth):
            self.c(i).wait_send()
        for k in range(self.depth):
            self.y(k).wait_send()
        for k in range(1, self.depth):
            self.z(k).wait_send()


def second_kernel(depth, hidden_blocks, slots, block, *refs):
    (hidden, grad_gate, grad_up, at_gate, at_up, at_down, gate_hbm, up_hbm, down_hbm) = refs[:9]
    (outputs, grad_tokens) = refs[9:11]
    (first, second, held_out, held_grad, load_sems) = refs[11:16]
    out_bufs, grad_bufs = refs[16:28], refs[28:40]
    per_shard = slots // (depth * ROWS * CORES)
    down_loads = load_copies(down_hbm, first, load_sems.at[0], hidden_blocks, slots)
    gate_loads = load_copies(gate_hbm, second, load_sems.at[1], hidden_blocks, slots)
    up_loads = load_copies(up_hbm, first, load_sems.at[2], hidden_blocks, slots)
    for load in down_loads + gate_loads:
        load.start()
    first[hidden_blocks * slots] = jnp.zeros((block, block), first.dtype)
    second[hidden_blocks * slots] = jnp.zeros((block, block), second.dtype)
    greet(depth)

    def wide(ref):
        return jnp.concatenate([ref[h] for h in range(hidden_blocks)], axis=1)

    def out_partial(shard):
        parts = []
        for j in range(0, per_shard, 2):
            place = shard * per_shard + j
            rows = [
                jnp.concatenate([first[at_down[h, place + i]] for i in range(2)], axis=1)
                for h in range(hidden_blocks)
            ]
            value = dot(wide(hidden), jnp.concatenate(rows, axis=0))
            parts.append((slice(j * block, (j + 2) * block), value))
        return parts

    def grad_partial(shard):
        parts = []
        for j in range(0, per_shard, 2):
            place = shard * per_shard + j
            value = None
            for left, buffer, at in ((grad_gate, second, at_gate), (grad_up, first, at_up)):
                rows = [
                    jnp.concatenate([buffer[at[h, place + i]] for h in range(hidden_blocks)], axis=1)
                    for i in range(2)
                ]
                term = dot(wide(left), jnp.concatenate(rows, axis=0), 1)
                value = term if value is None else value + term
            parts.append((slice(j * block, (j + 2) * block), value))
        return parts

    out = Scatter(depth, out_partial, held_out, out_bufs)
    grad = Scatter(depth, grad_partial, held_grad, grad_bufs)
    for load in down_loads:
        load.wait()
    each(0, depth, lambda k: out.sibling(k, True))
    each(0, depth, out.across)
    each(0, depth, lambda k: out.sibling(k, False))
    each(0, depth, out.keep)
    for load in up_loads:
        load.start()
    for load in gate_loads + up_loads:
        load.wait()
    each(0, depth, lambda k: grad.sibling(k, True))
    each(0, depth, grad.across)
    each(1, depth, out.along)
    each(0, depth, lambda k: grad.sibling(k, False))
    each(0, depth, grad.keep)
    each(1, depth, grad.along)
    out.result(outputs)
    grad.result(grad_tokens)
    out.finish()
    grad.finish()


def fused_body(depth, tokens, grad_out, gate_blocks, gate_index, gate_count, up_blocks, up_index, up_count, down_blocks, down_index, down_count):
    hidden_blocks, slots = gate_index.shape
    block = gate_blocks.shape[-1]
    rows, shard = tokens.shape
    devices = depth * ROWS * CORES
    kind = tokens.dtype
    at = [
        places(gate_index, gate_count),
        places(up_index, up_count),
        places(down_index, down_count),
    ]
    vmem = pl.BlockSpec(memory_space=pltpu.VMEM)
    smem = pl.BlockSpec(memory_space=pltpu.SMEM)
    anywhere = pl.BlockSpec(memory_space=pl.ANY)
    dma = pltpu.SemaphoreType.DMA
    weights = pltpu.VMEM((hidden_blocks * slots + 1, block, block), gate_blocks.dtype)
    gather_sems = [dma((n,)) for n in (depth, depth, depth, depth, 2 * depth, 2 * depth)]
    thin = jax.ShapeDtypeStruct((hidden_blocks, rows, block), jnp.bfloat16)
    flops = 2 * rows * shard * devices * hidden_blocks * block * 3
    cost = pl.CostEstimate(flops=flops, bytes_accessed=3 * gate_blocks.size * 2, transcendentals=0)
    hidden, grad_gate, grad_up = pl.pallas_call(
        functools.partial(first_kernel, depth, hidden_blocks, slots, block),
        out_shape=[thin] * 3,
        in_specs=[vmem] * 2 + [smem] * 3 + [anywhere] * 3,
        out_specs=[vmem] * 3,
        scratch_shapes=[
            weights,
            weights,
            pltpu.VMEM((devices, rows, shard), kind),
            pltpu.VMEM((devices, rows, shard), kind),
            pltpu.VMEM((hidden_blocks, rows, 2 * block), jnp.float32),
            pltpu.VMEM((hidden_blocks // 2, rows, 2 * block), jnp.float32),
            dma((3, hidden_blocks)),
        ]
        + gather_sems
        + gather_sems,
        compiler_params=pltpu.CompilerParams(
            collective_id=0, has_side_effects=True, vmem_limit_bytes=VMEM_LIMIT
        ),
        cost_estimate=cost,
        name="gather_and_project",
    )(tokens, grad_out, *at, gate_blocks, up_blocks, down_blocks)
    scatter_bufs = [
        pltpu.VMEM((n, rows, shard), jnp.bfloat16)
        for n in (2 * depth, 2 * depth, depth, depth, depth, depth)
    ]
    scatter_sems = [dma((n,)) for n in (2 * depth, 2 * depth, depth, depth, depth, depth)]
    held = pltpu.VMEM((depth, rows, shard), jnp.float32)
    result = jax.ShapeDtypeStruct((rows, shard), jnp.bfloat16)
    return pl.pallas_call(
        functools.partial(second_kernel, depth, hidden_blocks, slots, block),
        out_shape=[result] * 2,
        in_specs=[vmem] * 3 + [smem] * 3 + [anywhere] * 3,
        out_specs=[vmem] * 2,
        scratch_shapes=[weights, weights, held, held, dma((3, hidden_blocks))]
        + (scatter_bufs + scatter_sems) * 2,
        compiler_params=pltpu.CompilerParams(
            collective_id=1, has_side_effects=True, vmem_limit_bytes=VMEM_LIMIT
        ),
        cost_estimate=cost,
        name="expand_and_scatter",
    )(hidden, grad_gate, grad_up, *at, gate_blocks, up_blocks, down_blocks)


def fits(mesh, tokens, gate_index, gate_blocks):
    tp, dp = mesh.shape["tp"], mesh.shape["dp"]
    rows, shard = tokens.shape[0] // dp, tokens.shape[1] // tp
    hidden_blocks, slots = gate_index.shape[0] // tp, gate_index.shape[1]
    block = gate_blocks.shape[-1]
    held = hidden_blocks * slots * block * block * 2 * 2 + 2 * rows * tokens.shape[1] * 5
    return (
        tp % (CORES * ROWS) == 0
        and tp > CORES * ROWS
        and shard % (2 * block) == 0
        and hidden_blocks % 2 == 0
        and rows % 16 == 0
        and held <= VMEM_LIMIT
    )


def densify(blocks, index, count):
    hidden_blocks, slots = index.shape
    block = blocks.shape[-1]
    live = lax.broadcasted_iota(jnp.int32, (hidden_blocks, slots), 1) < count[:, None]
    places = lax.broadcasted_iota(jnp.int32, (hidden_blocks, slots, slots), 2)
    onehot = ((index[:, :, None] == places) & live[:, :, None]).astype(jnp.bfloat16)
    shaped = blocks.reshape(hidden_blocks, slots, block, block)
    return jnp.einsum("hsr,hsab->hrab", onehot, shaped, preferred_element_type=jnp.float32).astype(
        jnp.bfloat16
    )


def column_matrix(dense):
    hidden_blocks, slots, block, _ = dense.shape
    return dense.transpose(1, 2, 0, 3).reshape(slots * block, hidden_blocks * block)


def row_matrix(dense):
    hidden_blocks, slots, block, _ = dense.shape
    return dense.transpose(0, 2, 1, 3).reshape(hidden_blocks * block, slots * block)


def contract_last(left, right):
    return lax.dot_general(
        left, right, (((1,), (1,)), ((), ())), preferred_element_type=jnp.float32
    )


def body(
    tokens,
    grad_out,
    gate_blocks,
    gate_index,
    gate_count,
    up_blocks,
    up_index,
    up_count,
    down_blocks,
    down_index,
    down_count,
):
    hidden_blocks, slots = gate_index.shape
    block = gate_blocks.shape[-1]
    width = hidden_blocks * block
    gate_weight = column_matrix(densify(gate_blocks, gate_index, gate_count))
    up_weight = column_matrix(densify(up_blocks, up_index, up_count))
    down_weight = row_matrix(densify(down_blocks, down_index, down_count))
    all_tokens = lax.all_gather(tokens, "tp", axis=1, tiled=True)
    projected = jnp.concatenate(
        [
            jnp.dot(all_tokens, gate_weight, preferred_element_type=jnp.float32),
            jnp.dot(all_tokens, up_weight, preferred_element_type=jnp.float32),
        ],
        axis=1,
    )
    gate = projected[:, :width]
    upper = projected[:, width:]
    hidden = (gate * jax.nn.sigmoid(gate) * upper).astype(jnp.bfloat16)
    outputs = lax.psum_scatter(
        jnp.dot(hidden, down_weight, preferred_element_type=jnp.float32),
        "tp",
        scatter_dimension=1,
        tiled=True,
    )
    all_grads = lax.all_gather(grad_out, "tp", axis=1, tiled=True)
    grad_hidden = contract_last(all_grads, down_weight)
    gate = projected[:, :width]
    upper = projected[:, width:]
    sigma = jax.nn.sigmoid(gate)
    grad_gate = (grad_hidden * upper * sigma * (1.0 + gate * (1.0 - sigma))).astype(jnp.bfloat16)
    grad_up = (grad_hidden * gate * sigma).astype(jnp.bfloat16)
    grad_gate, grad_up = (grad_gate, grad_up)
    grad_tokens = lax.psum_scatter(
        contract_last(grad_gate, gate_weight) + contract_last(grad_up, up_weight),
        "tp",
        scatter_dimension=1,
        tiled=True,
    )
    return (outputs.astype(jnp.bfloat16), grad_tokens.astype(jnp.bfloat16))


def solution(mesh):
    placed = (
        P("dp", "tp"),
        P("dp", "tp"),
        P("tp", None, None),
        P("tp", None),
        P("tp"),
        P("tp", None, None),
        P("tp", None),
        P("tp"),
        P("tp", None, None),
        P("tp", None),
        P("tp"),
    )

    def run(*args):
        tokens, gate_blocks, gate_index = args[0], args[2], args[3]
        inner = body
        if fits(mesh, tokens, gate_index, gate_blocks):
            inner = functools.partial(fused_body, mesh.shape["tp"] // (CORES * ROWS))
        return jax.shard_map(
            inner, mesh=mesh, in_specs=placed, out_specs=(P("dp", "tp"), P("dp", "tp")), check_vma=False
        )(*args)

    return run
```

```python
import functools

import jax
import jax.numpy as jnp
from jax import lax
from jax.experimental import pallas as pl
from jax.experimental.pallas import tpu as pltpu
from jax.sharding import PartitionSpec as P


MESH = pl.DeviceIdType.MESH
CORES = 2
ROWS = 2
VMEM_LIMIT = 63 * 1024 * 1024


def places(index, count):
    hidden_blocks, slots = index.shape
    slot = lax.broadcasted_iota(jnp.int32, (hidden_blocks, slots, slots), 1)
    place = lax.broadcasted_iota(jnp.int32, (hidden_blocks, slots, slots), 2)
    where = jnp.sum(jnp.where(index[:, :, None] == place, slot, 0), axis=1)
    base = lax.broadcasted_iota(jnp.int32, (hidden_blocks, slots), 0) * slots
    return jnp.where(where < count[:, None], base + where, hidden_blocks * slots)


def position(depth):
    me = lax.axis_index("tp")
    core = lax.rem(me, CORES)
    row = lax.rem(me // CORES, ROWS)
    layer = me // (CORES * ROWS)
    return me, layer, row, core


def shard_of(layer, row, core):
    return (layer * ROWS + row) * CORES + core


def greet(depth):
    me, layer, row, core = position(depth)
    barrier = pltpu.get_barrier_semaphore()
    partners = [shard_of(layer, row, 1 - core), shard_of(layer, 1 - row, core)]
    partners += [shard_of(lax.rem(layer + k, depth), row, core) for k in range(1, depth)]
    for partner in partners:
        pl.semaphore_signal(barrier, inc=1, device_id={"tp": partner}, device_id_type=MESH)
    pl.semaphore_wait(barrier, len(partners))


def remote(src, dst, send, recv, target):
    return pltpu.make_async_remote_copy(
        src_ref=src,
        dst_ref=dst,
        send_sem=send,
        recv_sem=recv,
        device_id={"tp": target},
        device_id_type=MESH,
    )


def load_copies(hbm, buffer, sems, hidden_blocks, slots):
    return [
        pltpu.make_async_copy(
            hbm.at[pl.ds(h * slots, slots)], buffer.at[pl.ds(h * slots, slots)], sems.at[h]
        )
        for h in range(hidden_blocks)
    ]


def nearest(layer, depth, i):
    both = jnp.minimum(layer, depth - 1 - layer)
    down = jnp.where(2 * layer > depth - 1, layer - (i - both), layer + (i - both))
    step = (i + 1) // 2
    near = jnp.where(lax.rem(i, 2) == 1, layer - step, layer + step)
    return jnp.where(i <= 2 * both, near, down)


class Gather:
    def __init__(self, depth, full, sems):
        self.depth, self.full = depth, full
        self.z_send, self.z_recv, self.y_send, self.y_recv, self.c_send, self.c_recv = sems
        self.me, self.layer, self.row, self.core = position(depth)

    def at(self, i):
        return nearest(self.layer, self.depth, jnp.int32(i))

    def z(self, way, layer):
        block = self.full.at[shard_of(layer, self.row, self.core)]
        step = 1 if way == 0 else -1
        target = shard_of(lax.rem(self.layer + step + self.depth, self.depth), self.row, self.core)
        return remote(block, block, self.z_send.at[way, layer], self.z_recv.at[layer], target)

    def y(self, layer, row):
        block = self.full.at[shard_of(layer, row, self.core)]
        target = shard_of(self.layer, 1 - self.row, self.core)
        return remote(block, block, self.y_send.at[layer], self.y_recv.at[layer], target)

    def c(self, layer, row, core):
        block = self.full.at[shard_of(layer, row, core)]
        target = shard_of(self.layer, self.row, 1 - self.core)
        i = row * self.depth + layer
        return remote(block, block, self.c_send.at[i], self.c_recv.at[i], target)

    def hop(self, layer, act):
        @pl.when(jnp.logical_and(layer <= self.layer, self.layer < self.depth - 1))
        def _():
            act(self.z(0, layer))

        @pl.when(jnp.logical_and(layer >= self.layer, self.layer > 0))
        def _():
            act(self.z(1, layer))

    def spread(self, layer):
        self.hop(layer, lambda copy: copy.start())
        self.y(layer, self.row).start()
        self.c(layer, self.row, self.core).start()

    def from_layer(self, i):
        layer = self.at(i)
        self.z(0, layer).wait_recv()
        self.spread(layer)

    def from_row(self, i):
        layer = self.at(i)
        self.y(layer, 1 - self.row).wait_recv()
        self.c(layer, 1 - self.row, self.core).start()

    def chip(self, i, other):
        layer = self.at(i)
        row = 1 - self.row if other else self.row
        self.c(layer, row, 1 - self.core).wait_recv()
        return layer * ROWS + row

    def finish(self):
        def one(layer):
            self.hop(layer, lambda copy: copy.wait_send())
            self.y(layer, self.row).wait_send()
            for row in range(ROWS):
                self.c(layer, row, self.core).wait_send()

        each(0, self.depth, one)


def each(low, high, step):
    def run(k, carry):
        step(k)
        return carry

    lax.fori_loop(low, high, run, 0)


def dot(left, right, contract=0):
    return lax.dot_general(
        left, right, (((1,), (contract,)), ((), ())), preferred_element_type=jnp.float32
    )


def first_kernel(depth, hidden_blocks, slots, block, *refs):
    (tokens, grads, at_gate, at_up, at_down, gate_hbm, up_hbm, down_hbm) = refs[:8]
    (hidden, grad_gate, grad_up) = refs[8:11]
    (first, second, third, all_tokens, all_grads, projected, grad_hidden, load_sems) = refs[11:19]
    token_sems, grad_sems = refs[19:25], refs[25:31]
    me = position(depth)[0]
    per_chip = slots // (depth * ROWS)
    loads = load_copies(gate_hbm, first, load_sems.at[0], hidden_blocks, slots)
    loads += load_copies(up_hbm, second, load_sems.at[1], hidden_blocks, slots)
    down_loads = load_copies(down_hbm, third, load_sems.at[2], hidden_blocks, slots)
    for load in loads:
        load.start()
    all_tokens[me] = tokens[...]
    all_grads[me] = grads[...]
    greet(depth)
    tok = Gather(depth, all_tokens, token_sems)
    grd = Gather(depth, all_grads, grad_sems)
    tok.spread(tok.layer)
    first[hidden_blocks * slots] = jnp.zeros((block, block), first.dtype)
    second[hidden_blocks * slots] = jnp.zeros((block, block), second.dtype)
    third[hidden_blocks * slots] = jnp.zeros((block, block), third.dtype)
    projected[...] = jnp.zeros_like(projected)
    grad_hidden[...] = jnp.zeros_like(grad_hidden)
    for load in loads:
        load.wait()
    for load in down_loads:
        load.start()

    def pair(full, chip):
        return jnp.concatenate([full[CORES * chip + i] for i in range(CORES)], axis=1)

    def project(chip):
        def one(h):
            rows = [
                jnp.concatenate(
                    [first[at_gate[h, chip * per_chip + j]], second[at_up[h, chip * per_chip + j]]], axis=1
                )
                for j in range(per_chip)
            ]
            projected[h] += dot(pair(all_tokens, chip), jnp.concatenate(rows, axis=0))

        each(0, hidden_blocks, one)

    def push_back(chip):
        def one(p):
            rows = [
                jnp.concatenate(
                    [third[at_down[2 * p + i, chip * per_chip + j]] for j in range(per_chip)], axis=1
                )
                for i in range(2)
            ]
            grad_hidden[p] += dot(pair(all_grads, chip), jnp.concatenate(rows, axis=0), 1)

        each(0, hidden_blocks // 2, one)

    def activate(h):
        gate, up = projected[h][:, :block], projected[h][:, block:]
        hidden[h] = (gate * jax.nn.sigmoid(gate) * up).astype(hidden.dtype)

    def arrive(gather, work):
        gather.from_layer(1)
        gather.from_row(0)
        work(gather.chip(0, False))

        def step(i):
            gather.from_layer(i)
            gather.from_row(i - 1)
            work(gather.chip(i - 1, False))
            work(gather.chip(i - 2, True))

        each(2, depth, step)

    arrive(tok, project)
    grd.spread(grd.layer)
    project(tok.chip(depth - 1, False))
    project(tok.chip(depth - 2, True))
    tok.from_row(depth - 1)
    for load in down_loads:
        load.wait()
    project(tok.chip(depth - 1, True))
    arrive(grd, push_back)
    push_back(grd.chip(depth - 1, False))
    push_back(grd.chip(depth - 2, True))
    grd.from_row(depth - 1)
    each(0, hidden_blocks, activate)
    push_back(grd.chip(depth - 1, True))

    def back(p):
        for i in range(2):
            h = 2 * p + i
            gate, up = projected[h][:, :block], projected[h][:, block:]
            flow = grad_hidden[p][:, i * block : (i + 1) * block]
            sigma = jax.nn.sigmoid(gate)
            grad_gate[h] = (flow * up * sigma * (1.0 + gate * (1.0 - sigma))).astype(grad_gate.dtype)
            grad_up[h] = (flow * gate * sigma).astype(grad_up.dtype)

    each(0, hidden_blocks // 2, back)
    tok.finish()
    grd.finish()


class Scatter:
    def __init__(self, depth, partial, held, bufs):
        self.depth, self.partial, self.held = depth, partial, held
        (self.c_out, self.c_in, self.y_out, self.y_in, self.z_out, self.z_in) = bufs[:6]
        (self.c_send, self.c_recv, self.y_send, self.y_recv, self.z_send, self.z_recv) = bufs[6:]
        self.me, self.layer, self.row, self.core = position(depth)

    def far(self, n):
        return nearest(self.layer, self.depth, jnp.int32(self.depth - 1 - n))

    def c(self, i):
        target = shard_of(self.layer, self.row, 1 - self.core)
        return remote(self.c_out.at[i], self.c_in.at[i], self.c_send.at[i], self.c_recv.at[i], target)

    def y(self, n):
        layer = self.far(n)
        target = shard_of(self.layer, 1 - self.row, self.core)
        return remote(
            self.y_out.at[layer], self.y_in.at[layer], self.y_send.at[layer], self.y_recv.at[layer], target
        )

    def z(self, layer):
        up = layer > self.layer
        step = jnp.where(up, 1, -1)
        neighbour = lax.rem(self.layer + step + self.depth, self.depth)
        place = jnp.where(jnp.logical_and(layer == neighbour, step < 0), self.depth, layer)
        target = shard_of(neighbour, self.row, self.core)
        return remote(
            self.z_out.at[layer], self.z_in.at[place], self.z_send.at[layer], self.z_recv.at[place], target
        )

    def arrival(self, place):
        block = self.z_in.at[place]
        target = shard_of(self.layer, self.row, 1 - self.core)
        return remote(block, block, self.z_send.at[0], self.z_recv.at[place], target)

    def sibling(self, n, other):
        layer = self.far(n)
        row = 1 - self.row if other else self.row
        i = layer if other else self.depth + layer
        for cols, value in self.partial(shard_of(layer, row, 1 - self.core)):
            self.c_out[i, :, cols] = value.astype(self.c_out.dtype)
        self.c(i).start()

    def across(self, n):
        layer = self.far(n)
        parts = self.partial(shard_of(layer, 1 - self.row, self.core))
        self.c(layer).wait_recv()
        for cols, value in parts:
            total = value + self.c_in[layer, :, cols].astype(jnp.float32)
            self.y_out[layer, :, cols] = total.astype(self.y_out.dtype)

    def send_row(self, n):
        if n >= 2:
            self.y(n - 2).wait_send()
        self.y(n).start()

    def keep(self, n):
        layer = self.far(n)
        parts = self.partial(shard_of(layer, self.row, self.core))
        self.c(self.depth + layer).wait_recv()
        for cols, value in parts:
            self.held[layer, :, cols] = value + self.c_in[self.depth + layer, :, cols].astype(jnp.float32)

    def along(self, n):
        layer = self.far(n)
        self.y(n).wait_recv()
        self.held[layer] = self.held[layer] + self.y_in[layer].astype(jnp.float32)
        inner = jnp.logical_and(self.layer > 0, self.layer < self.depth - 1)

        @pl.when(inner)
        def _():
            self.arrival(layer).wait_recv()
            self.held[layer] = self.held[layer] + self.z_in[layer].astype(jnp.float32)

        self.z_out[layer] = self.held[layer].astype(self.z_out.dtype)
        self.z(layer).start()

    def result(self, out):
        last = self.depth - 1
        self.y(last).wait_recv()
        mine = self.layer
        self.held[mine] = self.held[mine] + self.y_in[mine].astype(jnp.float32)

        @pl.when(self.layer > 0)
        def _():
            self.arrival(mine).wait_recv()
            self.held[mine] = self.held[mine] + self.z_in[mine].astype(jnp.float32)

        @pl.when(self.layer < self.depth - 1)
        def _():
            self.arrival(self.depth).wait_recv()
            self.held[mine] = self.held[mine] + self.z_in[self.depth].astype(jnp.float32)

        out[...] = self.held[mine].astype(out.dtype)

    def finish(self):
        for i in range(2 * self.depth):
            self.c(i).wait_send()
        for n in range(max(self.depth - 2, 0), self.depth):
            self.y(n).wait_send()
        for n in range(self.depth - 1):
            self.z(self.far(n)).wait_send()


def second_kernel(depth, hidden_blocks, slots, block, *refs):
    (hidden, grad_gate, grad_up, at_gate, at_up, at_down, gate_hbm, up_hbm, down_hbm) = refs[:9]
    (outputs, grad_tokens) = refs[9:11]
    (first, second, held_out, held_grad, load_sems) = refs[11:16]
    out_bufs, grad_bufs = refs[16:28], refs[28:40]
    per_shard = slots // (depth * ROWS * CORES)
    down_loads = load_copies(down_hbm, first, load_sems.at[0], hidden_blocks, slots)
    gate_loads = load_copies(gate_hbm, second, load_sems.at[1], hidden_blocks, slots)
    up_loads = load_copies(up_hbm, first, load_sems.at[2], hidden_blocks, slots)
    for load in down_loads:
        load.start()
    first[hidden_blocks * slots] = jnp.zeros((block, block), first.dtype)
    second[hidden_blocks * slots] = jnp.zeros((block, block), second.dtype)
    greet(depth)

    def wide(ref):
        return jnp.concatenate([ref[h] for h in range(hidden_blocks)], axis=1)

    def out_partial(shard):
        parts = []
        for j in range(0, per_shard, 2):
            place = shard * per_shard + j
            rows = [
                jnp.concatenate([first[at_down[h, place + i]] for i in range(2)], axis=1)
                for h in range(hidden_blocks)
            ]
            value = dot(wide(hidden), jnp.concatenate(rows, axis=0))
            parts.append((slice(j * block, (j + 2) * block), value))
        return parts

    def grad_partial(shard):
        parts = []
        for j in range(0, per_shard, 2):
            place = shard * per_shard + j
            value = None
            for left, buffer, at in ((grad_gate, second, at_gate), (grad_up, first, at_up)):
                rows = [
                    jnp.concatenate([buffer[at[h, place + i]] for h in range(hidden_blocks)], axis=1)
                    for i in range(2)
                ]
                term = dot(wide(left), jnp.concatenate(rows, axis=0), 1)
                value = term if value is None else value + term
            parts.append((slice(j * block, (j + 2) * block), value))
        return parts

    out = Scatter(depth, out_partial, held_out, out_bufs)
    grad = Scatter(depth, grad_partial, held_grad, grad_bufs)
    for load in down_loads:
        load.wait()
    for load in gate_loads:
        load.start()
    each(0, depth, lambda n: out.sibling(n, True))
    each(0, depth, out.across)
    out.send_row(0)
    out.send_row(1)
    each(0, depth, lambda n: out.sibling(n, False))
    each(0, depth, out.keep)
    for load in up_loads:
        load.start()
    for load in gate_loads + up_loads:
        load.wait()
    each(0, depth, lambda n: grad.sibling(n, True))
    out.send_row(2)
    out.along(0)
    each(0, depth, grad.across)
    for n in range(3, depth):
        out.send_row(n)
        out.along(n - 2)
    grad.send_row(0)
    each(0, depth, lambda n: grad.sibling(n, False))
    out.along(depth - 2)
    grad.send_row(1)
    each(0, depth, grad.keep)
    for n in range(2, depth):
        grad.send_row(n)
        grad.along(n - 2)
    out.result(outputs)
    grad.along(depth - 2)
    grad.result(grad_tokens)
    out.finish()
    grad.finish()


def fused_body(depth, tokens, grad_out, gate_blocks, gate_index, gate_count, up_blocks, up_index, up_count, down_blocks, down_index, down_count):
    hidden_blocks, slots = gate_index.shape
    block = gate_blocks.shape[-1]
    rows, shard = tokens.shape
    devices = depth * ROWS * CORES
    kind = tokens.dtype
    at = [
        places(gate_index, gate_count),
        places(up_index, up_count),
        places(down_index, down_count),
    ]
    vmem = pl.BlockSpec(memory_space=pltpu.VMEM)
    smem = pl.BlockSpec(memory_space=pltpu.SMEM)
    anywhere = pl.BlockSpec(memory_space=pl.ANY)
    dma = pltpu.SemaphoreType.DMA
    weights = pltpu.VMEM((hidden_blocks * slots + 1, block, block), gate_blocks.dtype)
    gather_sems = [dma((2, depth))]
    gather_sems += [dma((n,)) for n in (depth, depth, depth, 2 * depth, 2 * depth)]
    thin = jax.ShapeDtypeStruct((hidden_blocks, rows, block), jnp.bfloat16)
    flops = 2 * rows * shard * devices * hidden_blocks * block * 3
    cost = pl.CostEstimate(flops=flops, bytes_accessed=3 * gate_blocks.size * 2, transcendentals=0)
    hidden, grad_gate, grad_up = pl.pallas_call(
        functools.partial(first_kernel, depth, hidden_blocks, slots, block),
        out_shape=[thin] * 3,
        in_specs=[vmem] * 2 + [smem] * 3 + [anywhere] * 3,
        out_specs=[vmem] * 3,
        scratch_shapes=[
            weights,
            weights,
            weights,
            pltpu.VMEM((devices, rows, shard), kind),
            pltpu.VMEM((devices, rows, shard), kind),
            pltpu.VMEM((hidden_blocks, rows, 2 * block), jnp.float32),
            pltpu.VMEM((hidden_blocks // 2, rows, 2 * block), jnp.float32),
            dma((3, hidden_blocks)),
        ]
        + gather_sems
        + gather_sems,
        compiler_params=pltpu.CompilerParams(
            collective_id=0, has_side_effects=True, vmem_limit_bytes=VMEM_LIMIT
        ),
        cost_estimate=cost,
        name="gather_and_project",
    )(tokens, grad_out, *at, gate_blocks, up_blocks, down_blocks)
    scatter_bufs = [
        pltpu.VMEM((n, rows, shard), jnp.bfloat16)
        for n in (2 * depth, 2 * depth, depth, depth, depth, depth + 1)
    ]
    scatter_sems = [dma((n,)) for n in (2 * depth, 2 * depth, depth, depth, depth, depth + 1)]
    held = pltpu.VMEM((depth, rows, shard), jnp.float32)
    result = jax.ShapeDtypeStruct((rows, shard), jnp.bfloat16)
    return pl.pallas_call(
        functools.partial(second_kernel, depth, hidden_blocks, slots, block),
        out_shape=[result] * 2,
        in_specs=[vmem] * 3 + [smem] * 3 + [anywhere] * 3,
        out_specs=[vmem] * 2,
        scratch_shapes=[weights, weights, held, held, dma((3, hidden_blocks))]
        + (scatter_bufs + scatter_sems) * 2,
        compiler_params=pltpu.CompilerParams(
            collective_id=1, has_side_effects=True, vmem_limit_bytes=VMEM_LIMIT
        ),
        cost_estimate=cost,
        name="expand_and_scatter",
    )(hidden, grad_gate, grad_up, *at, gate_blocks, up_blocks, down_blocks)


def fits(mesh, tokens, gate_index, gate_blocks):
    tp, dp = mesh.shape["tp"], mesh.shape["dp"]
    rows, shard = tokens.shape[0] // dp, tokens.shape[1] // tp
    hidden_blocks, slots = gate_index.shape[0] // tp, gate_index.shape[1]
    block = gate_blocks.shape[-1]
    held = hidden_blocks * slots * block * block * 2 * 3 + 2 * rows * tokens.shape[1] * 3
    return (
        tp % (CORES * ROWS) == 0
        and tp >= 3 * CORES * ROWS
        and shard % (2 * block) == 0
        and hidden_blocks % 2 == 0
        and rows % 16 == 0
        and held <= VMEM_LIMIT
    )


def densify(blocks, index, count):
    hidden_blocks, slots = index.shape
    block = blocks.shape[-1]
    live = lax.broadcasted_iota(jnp.int32, (hidden_blocks, slots), 1) < count[:, None]
    places = lax.broadcasted_iota(jnp.int32, (hidden_blocks, slots, slots), 2)
    onehot = ((index[:, :, None] == places) & live[:, :, None]).astype(jnp.bfloat16)
    shaped = blocks.reshape(hidden_blocks, slots, block, block)
    return jnp.einsum("hsr,hsab->hrab", onehot, shaped, preferred_element_type=jnp.float32).astype(
        jnp.bfloat16
    )


def column_matrix(dense):
    hidden_blocks, slots, block, _ = dense.shape
    return dense.transpose(1, 2, 0, 3).reshape(slots * block, hidden_blocks * block)


def row_matrix(dense):
    hidden_blocks, slots, block, _ = dense.shape
    return dense.transpose(0, 2, 1, 3).reshape(hidden_blocks * block, slots * block)


def contract_last(left, right):
    return lax.dot_general(
        left, right, (((1,), (1,)), ((), ())), preferred_element_type=jnp.float32
    )


def body(
    tokens,
    grad_out,
    gate_blocks,
    gate_index,
    gate_count,
    up_blocks,
    up_index,
    up_count,
    down_blocks,
    down_index,
    down_count,
):
    hidden_blocks, slots = gate_index.shape
    block = gate_blocks.shape[-1]
    width = hidden_blocks * block
    gate_weight = column_matrix(densify(gate_blocks, gate_index, gate_count))
    up_weight = column_matrix(densify(up_blocks, up_index, up_count))
    down_weight = row_matrix(densify(down_blocks, down_index, down_count))
    all_tokens = lax.all_gather(tokens, "tp", axis=1, tiled=True)
    projected = jnp.concatenate(
        [
            jnp.dot(all_tokens, gate_weight, preferred_element_type=jnp.float32),
            jnp.dot(all_tokens, up_weight, preferred_element_type=jnp.float32),
        ],
        axis=1,
    )
    gate = projected[:, :width]
    upper = projected[:, width:]
    hidden = (gate * jax.nn.sigmoid(gate) * upper).astype(jnp.bfloat16)
    outputs = lax.psum_scatter(
        jnp.dot(hidden, down_weight, preferred_element_type=jnp.float32),
        "tp",
        scatter_dimension=1,
        tiled=True,
    )
    all_grads = lax.all_gather(grad_out, "tp", axis=1, tiled=True)
    grad_hidden = contract_last(all_grads, down_weight)
    gate = projected[:, :width]
    upper = projected[:, width:]
    sigma = jax.nn.sigmoid(gate)
    grad_gate = (grad_hidden * upper * sigma * (1.0 + gate * (1.0 - sigma))).astype(jnp.bfloat16)
    grad_up = (grad_hidden * gate * sigma).astype(jnp.bfloat16)
    grad_gate, grad_up = (grad_gate, grad_up)
    grad_tokens = lax.psum_scatter(
        contract_last(grad_gate, gate_weight) + contract_last(grad_up, up_weight),
        "tp",
        scatter_dimension=1,
        tiled=True,
    )
    return (outputs.astype(jnp.bfloat16), grad_tokens.astype(jnp.bfloat16))


def solution(mesh):
    placed = (
        P("dp", "tp"),
        P("dp", "tp"),
        P("tp", None, None),
        P("tp", None),
        P("tp"),
        P("tp", None, None),
        P("tp", None),
        P("tp"),
        P("tp", None, None),
        P("tp", None),
        P("tp"),
    )

    def run(*args):
        tokens, gate_blocks, gate_index = args[0], args[2], args[3]
        inner = body
        if fits(mesh, tokens, gate_index, gate_blocks):
            inner = functools.partial(fused_body, mesh.shape["tp"] // (CORES * ROWS))
        return jax.shard_map(
            inner, mesh=mesh, in_specs=placed, out_specs=(P("dp", "tp"), P("dp", "tp")), check_vma=False
        )(*args)

    return run
```

```python
import functools

import jax
import jax.numpy as jnp
from jax import lax
from jax.experimental import pallas as pl
from jax.experimental.pallas import tpu as pltpu
from jax.sharding import PartitionSpec as P


MESH = pl.DeviceIdType.MESH
CORES = 2
ROWS = 2
VMEM_LIMIT = 63 * 1024 * 1024


def places(index, count):
    weights, hidden_blocks, slots = index.shape
    cube = (weights, hidden_blocks, slots, slots)
    slot = lax.broadcasted_iota(jnp.int32, cube, 2)
    place = lax.broadcasted_iota(jnp.int32, cube, 3)
    where = jnp.sum(jnp.where(index[..., None] == place, slot, 0), axis=2)
    base = lax.broadcasted_iota(jnp.int32, index.shape, 1) * slots
    return jnp.where(where < count[..., None], base + where, hidden_blocks * slots)


def position(depth):
    me = lax.axis_index("tp")
    core = lax.rem(me, CORES)
    row = lax.rem(me // CORES, ROWS)
    layer = me // (CORES * ROWS)
    return me, layer, row, core


def shard_of(layer, row, core):
    return (layer * ROWS + row) * CORES + core


def greet(depth):
    me, layer, row, core = position(depth)
    barrier = pltpu.get_barrier_semaphore()
    partners = [shard_of(layer, row, 1 - core), shard_of(layer, 1 - row, core)]
    partners += [shard_of(lax.rem(layer + k, depth), row, core) for k in range(1, depth)]
    for partner in partners:
        pl.semaphore_signal(barrier, inc=1, device_id={"tp": partner}, device_id_type=MESH)
    pl.semaphore_wait(barrier, len(partners))


def remote(src, dst, send, recv, target):
    return pltpu.make_async_remote_copy(
        src_ref=src,
        dst_ref=dst,
        send_sem=send,
        recv_sem=recv,
        device_id={"tp": target},
        device_id_type=MESH,
    )


def load_copies(hbm, buffer, sems, hidden_blocks, slots):
    return [
        pltpu.make_async_copy(
            hbm.at[pl.ds(h * slots, slots)], buffer.at[pl.ds(h * slots, slots)], sems.at[h]
        )
        for h in range(hidden_blocks)
    ]


def nearest(layer, depth, i):
    both = jnp.minimum(layer, depth - 1 - layer)
    down = jnp.where(2 * layer > depth - 1, layer - (i - both), layer + (i - both))
    step = (i + 1) // 2
    near = jnp.where(lax.rem(i, 2) == 1, layer - step, layer + step)
    return jnp.where(i <= 2 * both, near, down)


class Gather:
    def __init__(self, depth, full, sems):
        self.depth, self.full = depth, full
        self.z_send, self.z_recv, self.y_send, self.y_recv, self.c_send, self.c_recv = sems
        self.me, self.layer, self.row, self.core = position(depth)

    def at(self, i):
        return nearest(self.layer, self.depth, jnp.int32(i))

    def z(self, way, layer):
        block = self.full.at[shard_of(layer, self.row, self.core)]
        step = 1 if way == 0 else -1
        target = shard_of(lax.rem(self.layer + step + self.depth, self.depth), self.row, self.core)
        return remote(block, block, self.z_send.at[way, layer], self.z_recv.at[layer], target)

    def y(self, layer, row):
        block = self.full.at[shard_of(layer, row, self.core)]
        target = shard_of(self.layer, 1 - self.row, self.core)
        return remote(block, block, self.y_send.at[layer], self.y_recv.at[layer], target)

    def c(self, layer, row, core):
        block = self.full.at[shard_of(layer, row, core)]
        target = shard_of(self.layer, self.row, 1 - self.core)
        i = row * self.depth + layer
        return remote(block, block, self.c_send.at[i], self.c_recv.at[i], target)

    def hop(self, layer, act):
        @pl.when(jnp.logical_and(layer <= self.layer, self.layer < self.depth - 1))
        def _():
            act(self.z(0, layer))

        @pl.when(jnp.logical_and(layer >= self.layer, self.layer > 0))
        def _():
            act(self.z(1, layer))

    def spread(self, layer):
        self.hop(layer, lambda copy: copy.start())
        self.y(layer, self.row).start()
        self.c(layer, self.row, self.core).start()

    def from_layer(self, i):
        layer = self.at(i)
        self.z(0, layer).wait_recv()
        self.spread(layer)

    def from_row(self, i):
        layer = self.at(i)
        self.y(layer, 1 - self.row).wait_recv()
        self.c(layer, 1 - self.row, self.core).start()

    def chip(self, i, other):
        layer = self.at(i)
        row = 1 - self.row if other else self.row
        self.c(layer, row, 1 - self.core).wait_recv()
        return layer * ROWS + row

    def finish(self):
        def one(layer):
            self.hop(layer, lambda copy: copy.wait_send())
            self.y(layer, self.row).wait_send()
            for row in range(ROWS):
                self.c(layer, row, self.core).wait_send()

        each(0, self.depth, one)


def each(low, high, step):
    def run(k, carry):
        step(k)
        return carry

    lax.fori_loop(low, high, run, 0)


def dot(left, right, contract=0):
    return lax.dot_general(
        left, right, (((1,), (contract,)), ((), ())), preferred_element_type=jnp.float32
    )


class Scatter:
    def __init__(self, depth, partial, held, bufs):
        self.depth, self.partial, self.held = depth, partial, held
        (self.c_out, self.c_in, self.y_out, self.y_in, self.z_out, self.z_in) = bufs[:6]
        (self.c_send, self.c_recv, self.y_send, self.y_recv, self.z_send, self.z_recv) = bufs[6:]
        self.me, self.layer, self.row, self.core = position(depth)

    def far(self, n):
        return nearest(self.layer, self.depth, jnp.int32(self.depth - 1 - n))

    def c(self, i):
        target = shard_of(self.layer, self.row, 1 - self.core)
        return remote(self.c_out.at[i], self.c_in.at[i], self.c_send.at[i], self.c_recv.at[i], target)

    def y(self, n):
        layer = self.far(n)
        target = shard_of(self.layer, 1 - self.row, self.core)
        return remote(
            self.y_out.at[layer], self.y_in.at[layer], self.y_send.at[layer], self.y_recv.at[layer], target
        )

    def z(self, layer):
        up = layer > self.layer
        step = jnp.where(up, 1, -1)
        neighbour = lax.rem(self.layer + step + self.depth, self.depth)
        place = jnp.where(jnp.logical_and(layer == neighbour, step < 0), self.depth, layer)
        target = shard_of(neighbour, self.row, self.core)
        return remote(
            self.z_out.at[layer], self.z_in.at[place], self.z_send.at[layer], self.z_recv.at[place], target
        )

    def arrival(self, place):
        block = self.z_in.at[place]
        target = shard_of(self.layer, self.row, 1 - self.core)
        return remote(block, block, self.z_send.at[0], self.z_recv.at[place], target)

    def sibling(self, n, other):
        layer = self.far(n)
        row = 1 - self.row if other else self.row
        i = layer if other else self.depth + layer
        for cols, value in self.partial(shard_of(layer, row, 1 - self.core)):
            self.c_out[i, :, cols] = value.astype(self.c_out.dtype)
        self.c(i).start()

    def across(self, n):
        layer = self.far(n)
        parts = self.partial(shard_of(layer, 1 - self.row, self.core))
        self.c(layer).wait_recv()
        for cols, value in parts:
            total = value + self.c_in[layer, :, cols].astype(jnp.float32)
            self.y_out[layer, :, cols] = total.astype(self.y_out.dtype)

    def send_row(self, n):
        if n >= 2:
            self.y(n - 2).wait_send()
        self.y(n).start()

    def keep(self, n):
        layer = self.far(n)
        parts = self.partial(shard_of(layer, self.row, self.core))
        self.c(self.depth + layer).wait_recv()
        for cols, value in parts:
            self.held[layer, :, cols] = value + self.c_in[self.depth + layer, :, cols].astype(jnp.float32)

    def along(self, n):
        layer = self.far(n)
        self.y(n).wait_recv()
        self.held[layer] = self.held[layer] + self.y_in[layer].astype(jnp.float32)
        inner = jnp.logical_and(self.layer > 0, self.layer < self.depth - 1)

        @pl.when(inner)
        def _():
            self.arrival(layer).wait_recv()
            self.held[layer] = self.held[layer] + self.z_in[layer].astype(jnp.float32)

        self.z_out[layer] = self.held[layer].astype(self.z_out.dtype)
        self.z(layer).start()

    def result(self, out):
        last = self.depth - 1
        self.y(last).wait_recv()
        mine = self.layer
        self.held[mine] = self.held[mine] + self.y_in[mine].astype(jnp.float32)

        @pl.when(self.layer > 0)
        def _():
            self.arrival(mine).wait_recv()
            self.held[mine] = self.held[mine] + self.z_in[mine].astype(jnp.float32)

        @pl.when(self.layer < self.depth - 1)
        def _():
            self.arrival(self.depth).wait_recv()
            self.held[mine] = self.held[mine] + self.z_in[self.depth].astype(jnp.float32)

        out[...] = self.held[mine].astype(out.dtype)

    def finish(self):
        for i in range(2 * self.depth):
            self.c(i).wait_send()
        for n in range(max(self.depth - 2, 0), self.depth):
            self.y(n).wait_send()
        for n in range(self.depth - 1):
            self.z(self.far(n)).wait_send()


def layer_kernel(depth, hidden_blocks, slots, block, *refs):
    tokens, grads, at, gate_hbm, up_hbm, down_hbm, outputs, grad_tokens = refs[:8]
    (first, second, all_tokens, all_grads, projected, grad_hidden) = refs[8:14]
    (hidden, grad_gate, grad_up, held_out, held_grad, load_sems) = refs[14:20]
    token_sems, grad_sems = refs[20:26], refs[26:32]
    out_bufs, grad_bufs = refs[32:37], refs[37:40]
    out_sems, back_sems = refs[40:46], refs[46:52]
    me = position(depth)[0]
    per_chip = slots // (depth * ROWS)
    per_shard = per_chip // CORES
    zero = hidden_blocks * slots
    gate_loads = load_copies(gate_hbm, first, load_sems.at[0], hidden_blocks, slots)
    up_loads = load_copies(up_hbm, second, load_sems.at[1], hidden_blocks, slots)
    down_loads = load_copies(down_hbm, first, load_sems.at[2], hidden_blocks, slots)
    again_loads = load_copies(gate_hbm, first, load_sems.at[3], hidden_blocks, slots)
    for load in gate_loads + up_loads:
        load.start()
    all_tokens[me] = tokens[...]
    all_grads[me] = grads[...]
    greet(depth)
    tok = Gather(depth, all_tokens, token_sems)
    grd = Gather(depth, all_grads, grad_sems)
    tok.spread(tok.layer)
    first[zero] = jnp.zeros((block, block), first.dtype)
    second[zero] = jnp.zeros((block, block), second.dtype)
    projected[...] = jnp.zeros_like(projected)
    grad_hidden[...] = jnp.zeros_like(grad_hidden)

    def pair(full, chip):
        return jnp.concatenate([full[CORES * chip + i] for i in range(CORES)], axis=1)

    def project(chip):
        def one(h):
            rows = [
                jnp.concatenate(
                    [first[at[0, h, chip * per_chip + j]], second[at[1, h, chip * per_chip + j]]], axis=1
                )
                for j in range(per_chip)
            ]
            projected[h] += dot(pair(all_tokens, chip), jnp.concatenate(rows, axis=0))

        each(0, hidden_blocks, one)

    def push_back(chip):
        def one(p):
            rows = [
                jnp.concatenate(
                    [first[at[2, 2 * p + i, chip * per_chip + j]] for j in range(per_chip)], axis=1
                )
                for i in range(2)
            ]
            grad_hidden[p] += dot(pair(all_grads, chip), jnp.concatenate(rows, axis=0), 1)

        each(0, hidden_blocks // 2, one)

    def activate(h):
        gate, up = projected[h][:, :block], projected[h][:, block:]
        hidden[h] = (gate * jax.nn.sigmoid(gate) * up).astype(hidden.dtype)

    def back(p):
        for i in range(2):
            h = 2 * p + i
            gate, up = projected[h][:, :block], projected[h][:, block:]
            flow = grad_hidden[p][:, i * block : (i + 1) * block]
            sigma = jax.nn.sigmoid(gate)
            grad_gate[h] = (flow * up * sigma * (1.0 + gate * (1.0 - sigma))).astype(grad_gate.dtype)
            grad_up[h] = (flow * gate * sigma).astype(grad_up.dtype)

    def wide(ref):
        return jnp.concatenate([ref[h] for h in range(hidden_blocks)], axis=1)

    def out_partial(shard):
        parts = []
        for j in range(0, per_shard, 2):
            place = shard * per_shard + j
            rows = [
                jnp.concatenate([first[at[2, h, place + i]] for i in range(2)], axis=1)
                for h in range(hidden_blocks)
            ]
            value = dot(wide(hidden), jnp.concatenate(rows, axis=0))
            parts.append((slice(j * block, (j + 2) * block), value))
        return parts

    def grad_partial(shard):
        parts = []
        for j in range(0, per_shard, 2):
            place = shard * per_shard + j
            value = None
            for left, buffer, kind in ((grad_gate, first, 0), (grad_up, second, 1)):
                rows = [
                    jnp.concatenate([buffer[at[kind, h, place + i]] for h in range(hidden_blocks)], axis=1)
                    for i in range(2)
                ]
                term = dot(wide(left), jnp.concatenate(rows, axis=0), 1)
                value = term if value is None else value + term
            parts.append((slice(j * block, (j + 2) * block), value))
        return parts

    def arrive(gather, work, loads):
        gather.from_layer(1)
        gather.from_row(0)
        for load in loads:
            load.wait()
        work(gather.chip(0, False))

        def step(i):
            gather.from_layer(i)
            gather.from_row(i - 1)
            work(gather.chip(i - 1, False))
            work(gather.chip(i - 2, True))

        each(2, depth, step)

    last = depth - 1
    arrive(tok, project, gate_loads + up_loads)
    grd.spread(grd.layer)
    project(tok.chip(last, False))
    project(tok.chip(last - 1, True))
    tok.from_row(last)
    project(tok.chip(last, True))
    for load in down_loads:
        load.start()
    each(0, hidden_blocks, activate)
    arrive(grd, push_back, down_loads)

    tok.finish()
    out_stage = (all_tokens.at[pl.ds(0, 2 * depth)],) + out_bufs
    back_stage = (
        all_tokens.at[pl.ds(2 * depth, 2 * depth)],
        grad_bufs[0],
        all_grads.at[pl.ds(0, depth)],
        grad_bufs[1],
        all_grads.at[pl.ds(depth, depth)],
        grad_bufs[2],
    )
    out = Scatter(depth, out_partial, held_out, out_stage + out_sems)
    grad = Scatter(depth, grad_partial, held_grad, back_stage + back_sems)
    each(0, depth, lambda n: out.sibling(n, True))
    push_back(grd.chip(last, False))
    push_back(grd.chip(last - 1, True))
    each(0, depth, out.across)
    out.send_row(0)
    each(0, depth, lambda n: out.sibling(n, False))
    grd.from_row(last)
    out.send_row(1)
    each(0, depth, out.keep)
    push_back(grd.chip(last, True))
    for load in again_loads:
        load.start()
    each(0, hidden_blocks // 2, back)
    grd.finish()
    for load in again_loads:
        load.wait()
    each(0, depth, lambda n: grad.sibling(n, True))
    out.send_row(2)
    out.along(0)
    each(0, depth, grad.across)
    for n in range(3, depth):
        out.send_row(n)
        out.along(n - 2)
    grad.send_row(0)
    each(0, depth, lambda n: grad.sibling(n, False))
    out.along(depth - 2)
    grad.send_row(1)
    each(0, depth, grad.keep)
    for n in range(2, depth):
        grad.send_row(n)
        grad.along(n - 2)
    out.result(outputs)
    grad.along(depth - 2)
    grad.result(grad_tokens)
    out.finish()
    grad.finish()


def fused_body(depth, tokens, grad_out, gate_blocks, gate_index, gate_count, up_blocks, up_index, up_count, down_blocks, down_index, down_count):
    hidden_blocks, slots = gate_index.shape
    block = gate_blocks.shape[-1]
    rows, shard = tokens.shape
    devices = depth * ROWS * CORES
    at = places(
        jnp.stack([gate_index, up_index, down_index]), jnp.stack([gate_count, up_count, down_count])
    )
    vmem = pl.BlockSpec(memory_space=pltpu.VMEM)
    smem = pl.BlockSpec(memory_space=pltpu.SMEM)
    anywhere = pl.BlockSpec(memory_space=pl.ANY)
    dma = pltpu.SemaphoreType.DMA
    weights = pltpu.VMEM((hidden_blocks * slots + 1, block, block), gate_blocks.dtype)
    gather_sems = [dma((2, depth))]
    gather_sems += [dma((n,)) for n in (depth, depth, depth, 2 * depth, 2 * depth)]
    scatter_sems = [dma((n,)) for n in (2 * depth, 2 * depth, depth, depth, depth, depth + 1)]
    thin = pltpu.VMEM((hidden_blocks, rows, block), jnp.bfloat16)
    held = pltpu.VMEM((depth, rows, shard), jnp.float32)
    full = pltpu.VMEM((devices, rows, shard), tokens.dtype)
    sizes = (2 * depth, depth, depth, depth, depth + 1, 2 * depth, depth, depth + 1)
    result = jax.ShapeDtypeStruct((rows, shard), jnp.bfloat16)
    flops = 2 * rows * shard * devices * hidden_blocks * block * 6
    return pl.pallas_call(
        functools.partial(layer_kernel, depth, hidden_blocks, slots, block),
        out_shape=[result] * 2,
        in_specs=[vmem] * 2 + [smem] + [anywhere] * 3,
        out_specs=[vmem] * 2,
        scratch_shapes=[
            weights,
            weights,
            full,
            full,
            pltpu.VMEM((hidden_blocks, rows, 2 * block), jnp.float32),
            pltpu.VMEM((hidden_blocks // 2, rows, 2 * block), jnp.float32),
            thin,
            thin,
            thin,
            held,
            held,
            dma((4, hidden_blocks)),
        ]
        + gather_sems * 2
        + [pltpu.VMEM((n, rows, shard), jnp.bfloat16) for n in sizes]
        + scatter_sems * 2,
        compiler_params=pltpu.CompilerParams(
            collective_id=0, has_side_effects=True, vmem_limit_bytes=VMEM_LIMIT
        ),
        cost_estimate=pl.CostEstimate(
            flops=flops, bytes_accessed=4 * gate_blocks.size * 2, transcendentals=0
        ),
        name="block_pruned_layer",
    )(tokens, grad_out, at, gate_blocks, up_blocks, down_blocks)


def fits(mesh, tokens, gate_index, gate_blocks):
    tp, dp = mesh.shape["tp"], mesh.shape["dp"]
    rows, shard = tokens.shape[0] // dp, tokens.shape[1] // tp
    hidden_blocks, slots = gate_index.shape[0] // tp, gate_index.shape[1]
    block = gate_blocks.shape[-1]
    held = hidden_blocks * slots * block * block * 2 * 2 + 2 * rows * tokens.shape[1] * 6
    return (
        tp % (CORES * ROWS) == 0
        and tp >= 3 * CORES * ROWS
        and shard % (2 * block) == 0
        and hidden_blocks % 2 == 0
        and rows % 16 == 0
        and held <= VMEM_LIMIT
    )


def densify(blocks, index, count):
    hidden_blocks, slots = index.shape
    block = blocks.shape[-1]
    live = lax.broadcasted_iota(jnp.int32, (hidden_blocks, slots), 1) < count[:, None]
    places = lax.broadcasted_iota(jnp.int32, (hidden_blocks, slots, slots), 2)
    onehot = ((index[:, :, None] == places) & live[:, :, None]).astype(jnp.bfloat16)
    shaped = blocks.reshape(hidden_blocks, slots, block, block)
    return jnp.einsum("hsr,hsab->hrab", onehot, shaped, preferred_element_type=jnp.float32).astype(
        jnp.bfloat16
    )


def column_matrix(dense):
    hidden_blocks, slots, block, _ = dense.shape
    return dense.transpose(1, 2, 0, 3).reshape(slots * block, hidden_blocks * block)


def row_matrix(dense):
    hidden_blocks, slots, block, _ = dense.shape
    return dense.transpose(0, 2, 1, 3).reshape(hidden_blocks * block, slots * block)


def contract_last(left, right):
    return lax.dot_general(
        left, right, (((1,), (1,)), ((), ())), preferred_element_type=jnp.float32
    )


def body(
    tokens,
    grad_out,
    gate_blocks,
    gate_index,
    gate_count,
    up_blocks,
    up_index,
    up_count,
    down_blocks,
    down_index,
    down_count,
):
    hidden_blocks, slots = gate_index.shape
    block = gate_blocks.shape[-1]
    width = hidden_blocks * block
    gate_weight = column_matrix(densify(gate_blocks, gate_index, gate_count))
    up_weight = column_matrix(densify(up_blocks, up_index, up_count))
    down_weight = row_matrix(densify(down_blocks, down_index, down_count))
    all_tokens = lax.all_gather(tokens, "tp", axis=1, tiled=True)
    projected = jnp.concatenate(
        [
            jnp.dot(all_tokens, gate_weight, preferred_element_type=jnp.float32),
            jnp.dot(all_tokens, up_weight, preferred_element_type=jnp.float32),
        ],
        axis=1,
    )
    gate = projected[:, :width]
    upper = projected[:, width:]
    hidden = (gate * jax.nn.sigmoid(gate) * upper).astype(jnp.bfloat16)
    outputs = lax.psum_scatter(
        jnp.dot(hidden, down_weight, preferred_element_type=jnp.float32),
        "tp",
        scatter_dimension=1,
        tiled=True,
    )
    all_grads = lax.all_gather(grad_out, "tp", axis=1, tiled=True)
    grad_hidden = contract_last(all_grads, down_weight)
    gate = projected[:, :width]
    upper = projected[:, width:]
    sigma = jax.nn.sigmoid(gate)
    grad_gate = (grad_hidden * upper * sigma * (1.0 + gate * (1.0 - sigma))).astype(jnp.bfloat16)
    grad_up = (grad_hidden * gate * sigma).astype(jnp.bfloat16)
    grad_gate, grad_up = (grad_gate, grad_up)
    grad_tokens = lax.psum_scatter(
        contract_last(grad_gate, gate_weight) + contract_last(grad_up, up_weight),
        "tp",
        scatter_dimension=1,
        tiled=True,
    )
    return (outputs.astype(jnp.bfloat16), grad_tokens.astype(jnp.bfloat16))


def solution(mesh):
    placed = (
        P("dp", "tp"),
        P("dp", "tp"),
        P("tp", None, None),
        P("tp", None),
        P("tp"),
        P("tp", None, None),
        P("tp", None),
        P("tp"),
        P("tp", None, None),
        P("tp", None),
        P("tp"),
    )

    def run(*args):
        tokens, gate_blocks, gate_index = args[0], args[2], args[3]
        inner = body
        if fits(mesh, tokens, gate_index, gate_blocks):
            inner = functools.partial(fused_body, mesh.shape["tp"] // (CORES * ROWS))
        return jax.shard_map(
            inner, mesh=mesh, in_specs=placed, out_specs=(P("dp", "tp"), P("dp", "tp")), check_vma=False
        )(*args)

    return run
```

```python
import functools

import jax
import jax.numpy as jnp
from jax import lax
from jax.experimental import pallas as pl
from jax.experimental.pallas import tpu as pltpu
from jax.sharding import PartitionSpec as P


MESH = pl.DeviceIdType.MESH
CORES = 2
ROWS = 2
VMEM_LIMIT = 63 * 1024 * 1024


def places(index, count):
    weights, hidden_blocks, slots = index.shape
    cube = (weights, hidden_blocks, slots, slots)
    slot = lax.broadcasted_iota(jnp.int32, cube, 2)
    place = lax.broadcasted_iota(jnp.int32, cube, 3)
    where = jnp.sum(jnp.where(index[..., None] == place, slot, 0), axis=2)
    base = lax.broadcasted_iota(jnp.int32, index.shape, 1) * slots
    return jnp.where(where < count[..., None], base + where, hidden_blocks * slots)


def position(depth):
    me = lax.axis_index("tp")
    core = lax.rem(me, CORES)
    row = lax.rem(me // CORES, ROWS)
    layer = me // (CORES * ROWS)
    return me, layer, row, core


def shard_of(layer, row, core):
    return (layer * ROWS + row) * CORES + core


def greet(depth):
    me, layer, row, core = position(depth)
    barrier = pltpu.get_barrier_semaphore()
    partners = [shard_of(layer, row, 1 - core), shard_of(layer, 1 - row, core)]
    partners += [shard_of(lax.rem(layer + k, depth), row, core) for k in range(1, depth)]
    for partner in partners:
        pl.semaphore_signal(barrier, inc=1, device_id={"tp": partner}, device_id_type=MESH)
    pl.semaphore_wait(barrier, len(partners))


def remote(src, dst, send, recv, target):
    return pltpu.make_async_remote_copy(
        src_ref=src,
        dst_ref=dst,
        send_sem=send,
        recv_sem=recv,
        device_id={"tp": target},
        device_id_type=MESH,
    )


def load_copies(hbm, buffer, sems, hidden_blocks, slots):
    return [
        pltpu.make_async_copy(
            hbm.at[pl.ds(h * slots, slots)], buffer.at[pl.ds(h * slots, slots)], sems.at[h]
        )
        for h in range(hidden_blocks)
    ]


def nearest(layer, depth, i):
    both = jnp.minimum(layer, depth - 1 - layer)
    down = jnp.where(2 * layer > depth - 1, layer - (i - both), layer + (i - both))
    step = (i + 1) // 2
    near = jnp.where(lax.rem(i, 2) == 1, layer - step, layer + step)
    return jnp.where(i <= 2 * both, near, down)


class Gather:
    def __init__(self, depth, full, sems):
        self.depth, self.full = depth, full
        self.z_send, self.z_recv, self.y_send, self.y_recv, self.c_send, self.c_recv = sems
        self.me, self.layer, self.row, self.core = position(depth)

    def at(self, i):
        return nearest(self.layer, self.depth, jnp.int32(i))

    def z(self, way, layer):
        block = self.full.at[shard_of(layer, self.row, self.core)]
        step = 1 if way == 0 else -1
        target = shard_of(lax.rem(self.layer + step + self.depth, self.depth), self.row, self.core)
        return remote(block, block, self.z_send.at[way, layer], self.z_recv.at[layer], target)

    def y(self, layer, row):
        block = self.full.at[shard_of(layer, row, self.core)]
        target = shard_of(self.layer, 1 - self.row, self.core)
        return remote(block, block, self.y_send.at[layer], self.y_recv.at[layer], target)

    def c(self, layer, row, core):
        block = self.full.at[shard_of(layer, row, core)]
        target = shard_of(self.layer, self.row, 1 - self.core)
        i = row * self.depth + layer
        return remote(block, block, self.c_send.at[i], self.c_recv.at[i], target)

    def hop(self, layer, act):
        @pl.when(jnp.logical_and(layer <= self.layer, self.layer < self.depth - 1))
        def _():
            act(self.z(0, layer))

        @pl.when(jnp.logical_and(layer >= self.layer, self.layer > 0))
        def _():
            act(self.z(1, layer))

    def spread(self, layer):
        self.hop(layer, lambda copy: copy.start())
        self.y(layer, self.row).start()
        self.c(layer, self.row, self.core).start()

    def from_layer(self, i):
        layer = self.at(i)
        self.z(0, layer).wait_recv()
        self.spread(layer)

    def from_row(self, i):
        layer = self.at(i)
        self.y(layer, 1 - self.row).wait_recv()
        self.c(layer, 1 - self.row, self.core).start()

    def chip(self, i, other):
        layer = self.at(i)
        row = 1 - self.row if other else self.row
        self.c(layer, row, 1 - self.core).wait_recv()
        return layer * ROWS + row

    def finish(self):
        def one(layer):
            self.hop(layer, lambda copy: copy.wait_send())
            self.y(layer, self.row).wait_send()
            for row in range(ROWS):
                self.c(layer, row, self.core).wait_send()

        each(0, self.depth, one)


def each(low, high, step):
    def run(k, carry):
        step(k)
        return carry

    lax.fori_loop(low, high, run, 0)


def dot(left, right, contract=0):
    return lax.dot_general(
        left, right, (((1,), (contract,)), ((), ())), preferred_element_type=jnp.float32
    )


class Scatter:
    def __init__(self, depth, partial, held, bufs):
        self.depth, self.partial, self.held = depth, partial, held
        (self.c_out, self.c_in, self.y_out, self.y_in, self.z_out, self.z_in) = bufs[:6]
        (self.c_send, self.c_recv, self.y_send, self.y_recv, self.z_send, self.z_recv) = bufs[6:]
        self.me, self.layer, self.row, self.core = position(depth)

    def far(self, n):
        return nearest(self.layer, self.depth, jnp.int32(self.depth - 1 - n))

    def c(self, i):
        target = shard_of(self.layer, self.row, 1 - self.core)
        return remote(self.c_out.at[i], self.c_in.at[i], self.c_send.at[i], self.c_recv.at[i], target)

    def y(self, n):
        layer = self.far(n)
        target = shard_of(self.layer, 1 - self.row, self.core)
        return remote(
            self.y_out.at[layer], self.y_in.at[layer], self.y_send.at[layer], self.y_recv.at[layer], target
        )

    def z(self, layer):
        up = layer > self.layer
        step = jnp.where(up, 1, -1)
        neighbour = lax.rem(self.layer + step + self.depth, self.depth)
        place = jnp.where(jnp.logical_and(layer == neighbour, step < 0), self.depth, layer)
        target = shard_of(neighbour, self.row, self.core)
        return remote(
            self.z_out.at[layer], self.z_in.at[place], self.z_send.at[layer], self.z_recv.at[place], target
        )

    def arrival(self, place):
        block = self.z_in.at[place]
        target = shard_of(self.layer, self.row, 1 - self.core)
        return remote(block, block, self.z_send.at[0], self.z_recv.at[place], target)

    def sibling(self, n, other):
        layer = self.far(n)
        row = 1 - self.row if other else self.row
        i = layer if other else self.depth + layer
        for cols, value in self.partial(shard_of(layer, row, 1 - self.core)):
            self.c_out[i, :, cols] = value.astype(self.c_out.dtype)
        self.c(i).start()

    def across(self, n):
        layer = self.far(n)
        parts = self.partial(shard_of(layer, 1 - self.row, self.core))
        self.c(layer).wait_recv()
        for cols, value in parts:
            total = value + self.c_in[layer, :, cols].astype(jnp.float32)
            self.y_out[layer, :, cols] = total.astype(self.y_out.dtype)

    def hold_row(self, n):
        self.y(n - 2).wait_send()

    def send_row(self, n):
        self.y(n).start()

    def keep(self, n):
        layer = self.far(n)
        parts = self.partial(shard_of(layer, self.row, self.core))
        self.c(self.depth + layer).wait_recv()
        for cols, value in parts:
            self.held[layer, :, cols] = value + self.c_in[self.depth + layer, :, cols].astype(jnp.float32)

    def along(self, n):
        layer = self.far(n)
        self.y(n).wait_recv()
        self.held[layer] = self.held[layer] + self.y_in[layer].astype(jnp.float32)
        inner = jnp.logical_and(self.layer > 0, self.layer < self.depth - 1)

        @pl.when(inner)
        def _():
            self.arrival(layer).wait_recv()
            self.held[layer] = self.held[layer] + self.z_in[layer].astype(jnp.float32)

        self.z_out[layer] = self.held[layer].astype(self.z_out.dtype)
        self.z(layer).start()

    def result(self, out):
        last = self.depth - 1
        self.y(last).wait_recv()
        mine = self.layer
        self.held[mine] = self.held[mine] + self.y_in[mine].astype(jnp.float32)

        @pl.when(self.layer > 0)
        def _():
            self.arrival(mine).wait_recv()
            self.held[mine] = self.held[mine] + self.z_in[mine].astype(jnp.float32)

        @pl.when(self.layer < self.depth - 1)
        def _():
            self.arrival(self.depth).wait_recv()
            self.held[mine] = self.held[mine] + self.z_in[self.depth].astype(jnp.float32)

        out[...] = self.held[mine].astype(out.dtype)

    def finish(self, held):
        for i in range(2 * self.depth):
            self.c(i).wait_send()
        for n in range(held, self.depth):
            self.y(n).wait_send()
        for n in range(self.depth - 1):
            self.z(self.far(n)).wait_send()


def layer_kernel(depth, hidden_blocks, slots, block, *refs):
    tokens, grads, at, gate_hbm, up_hbm, down_hbm, outputs, grad_tokens = refs[:8]
    (first, second, all_tokens, all_grads, projected, grad_hidden) = refs[8:14]
    (hidden, grad_gate, grad_up, held_out, held_grad, load_sems) = refs[14:20]
    token_sems, grad_sems = refs[20:26], refs[26:32]
    out_bufs, grad_bufs = refs[32:37], refs[37:40]
    out_sems, back_sems = refs[40:46], refs[46:52]
    me = position(depth)[0]
    per_chip = slots // (depth * ROWS)
    per_shard = per_chip // CORES
    zero = hidden_blocks * slots
    gate_loads = load_copies(gate_hbm, first, load_sems.at[0], hidden_blocks, slots)
    up_loads = load_copies(up_hbm, second, load_sems.at[1], hidden_blocks, slots)
    down_loads = load_copies(down_hbm, first, load_sems.at[2], hidden_blocks, slots)
    again_loads = load_copies(gate_hbm, first, load_sems.at[3], hidden_blocks, slots)
    for load in gate_loads + up_loads:
        load.start()
    all_tokens[me] = tokens[...]
    all_grads[me] = grads[...]
    greet(depth)
    tok = Gather(depth, all_tokens, token_sems)
    grd = Gather(depth, all_grads, grad_sems)
    tok.spread(tok.layer)
    first[zero] = jnp.zeros((block, block), first.dtype)
    second[zero] = jnp.zeros((block, block), second.dtype)
    projected[...] = jnp.zeros_like(projected)
    grad_hidden[...] = jnp.zeros_like(grad_hidden)

    def pair(full, chip):
        return jnp.concatenate([full[CORES * chip + i] for i in range(CORES)], axis=1)

    def project(chip):
        def one(h):
            rows = [
                jnp.concatenate(
                    [first[at[0, h, chip * per_chip + j]], second[at[1, h, chip * per_chip + j]]], axis=1
                )
                for j in range(per_chip)
            ]
            projected[h] += dot(pair(all_tokens, chip), jnp.concatenate(rows, axis=0))

        each(0, hidden_blocks, one)

    def push_back(chip):
        def one(p):
            rows = [
                jnp.concatenate(
                    [first[at[2, 2 * p + i, chip * per_chip + j]] for j in range(per_chip)], axis=1
                )
                for i in range(2)
            ]
            grad_hidden[p] += dot(pair(all_grads, chip), jnp.concatenate(rows, axis=0), 1)

        each(0, hidden_blocks // 2, one)

    def activate(h):
        gate, up = projected[h][:, :block], projected[h][:, block:]
        hidden[h] = (gate * jax.nn.sigmoid(gate) * up).astype(hidden.dtype)

    def back(p):
        for i in range(2):
            h = 2 * p + i
            gate, up = projected[h][:, :block], projected[h][:, block:]
            flow = grad_hidden[p][:, i * block : (i + 1) * block]
            sigma = jax.nn.sigmoid(gate)
            grad_gate[h] = (flow * up * sigma * (1.0 + gate * (1.0 - sigma))).astype(grad_gate.dtype)
            grad_up[h] = (flow * gate * sigma).astype(grad_up.dtype)

    def wide(ref):
        return jnp.concatenate([ref[h] for h in range(hidden_blocks)], axis=1)

    def out_partial(shard):
        parts = []
        for j in range(0, per_shard, 2):
            place = shard * per_shard + j
            rows = [
                jnp.concatenate([first[at[2, h, place + i]] for i in range(2)], axis=1)
                for h in range(hidden_blocks)
            ]
            value = dot(wide(hidden), jnp.concatenate(rows, axis=0))
            parts.append((slice(j * block, (j + 2) * block), value))
        return parts

    def grad_partial(shard):
        parts = []
        for j in range(0, per_shard, 2):
            place = shard * per_shard + j
            value = None
            for left, buffer, kind in ((grad_gate, first, 0), (grad_up, second, 1)):
                rows = [
                    jnp.concatenate([buffer[at[kind, h, place + i]] for h in range(hidden_blocks)], axis=1)
                    for i in range(2)
                ]
                term = dot(wide(left), jnp.concatenate(rows, axis=0), 1)
                value = term if value is None else value + term
            parts.append((slice(j * block, (j + 2) * block), value))
        return parts

    last = depth - 1
    tok.from_layer(1)
    tok.from_row(0)
    for load in gate_loads + up_loads:
        load.wait()
    project(tok.chip(0, False))

    def token_step(i):
        tok.from_layer(i)
        tok.from_row(i - 1)
        project(tok.chip(i - 1, False))
        project(tok.chip(i - 2, True))

    each(2, depth, token_step)
    grd.spread(grd.layer)
    project(tok.chip(last, False))
    project(tok.chip(last - 1, True))
    grd.from_layer(1)
    tok.from_row(last)
    grd.from_row(0)
    project(tok.chip(last, True))
    for load in down_loads:
        load.start()
    grd.from_layer(2)
    grd.from_row(1)
    each(0, hidden_blocks, activate)
    for load in down_loads:
        load.wait()
    push_back(grd.chip(0, False))
    push_back(grd.chip(0, True))

    def grad_step(i):
        grd.from_layer(i)
        grd.from_row(i - 1)
        push_back(grd.chip(i - 2, False))
        push_back(grd.chip(i - 2, True))

    each(3, depth, grad_step)

    tok.finish()
    out_stage = (all_tokens.at[pl.ds(0, 2 * depth)],) + out_bufs
    back_stage = (
        all_tokens.at[pl.ds(2 * depth, 2 * depth)],
        grad_bufs[0],
        all_grads.at[pl.ds(0, depth)],
        grad_bufs[1],
        all_grads.at[pl.ds(depth, depth)],
        grad_bufs[2],
    )
    out = Scatter(depth, out_partial, held_out, out_stage + out_sems)
    grad = Scatter(depth, grad_partial, held_grad, back_stage + back_sems)
    each(0, depth, lambda n: out.sibling(n, True))
    push_back(grd.chip(last - 1, False))
    push_back(grd.chip(last - 1, True))
    push_back(grd.chip(last, False))
    each(0, depth, out.across)
    each(0, depth, out.send_row)
    each(0, depth, lambda n: out.sibling(n, False))
    grd.from_row(last)
    each(0, depth, out.keep)
    push_back(grd.chip(last, True))
    for load in again_loads:
        load.start()
    each(0, hidden_blocks // 2, back)
    grd.finish()
    out.along(0)
    for load in again_loads:
        load.wait()
    each(0, depth, lambda n: grad.sibling(n, True))
    each(0, depth, grad.across)
    grad.send_row(0)
    grad.send_row(1)
    out.along(1)
    each(0, depth, lambda n: grad.sibling(n, False))
    for n in range(2, depth - 1):
        out.along(n)
    each(0, depth, grad.keep)
    for n in range(2, depth):
        grad.hold_row(n)
        grad.send_row(n)
        grad.along(n - 2)
    out.result(outputs)
    grad.along(depth - 2)
    grad.result(grad_tokens)
    out.finish(0)
    grad.finish(depth - 2)


def fused_body(depth, tokens, grad_out, gate_blocks, gate_index, gate_count, up_blocks, up_index, up_count, down_blocks, down_index, down_count):
    hidden_blocks, slots = gate_index.shape
    block = gate_blocks.shape[-1]
    rows, shard = tokens.shape
    devices = depth * ROWS * CORES
    at = places(
        jnp.stack([gate_index, up_index, down_index]), jnp.stack([gate_count, up_count, down_count])
    )
    vmem = pl.BlockSpec(memory_space=pltpu.VMEM)
    smem = pl.BlockSpec(memory_space=pltpu.SMEM)
    anywhere = pl.BlockSpec(memory_space=pl.ANY)
    dma = pltpu.SemaphoreType.DMA
    weights = pltpu.VMEM((hidden_blocks * slots + 1, block, block), gate_blocks.dtype)
    gather_sems = [dma((2, depth))]
    gather_sems += [dma((n,)) for n in (depth, depth, depth, 2 * depth, 2 * depth)]
    scatter_sems = [dma((n,)) for n in (2 * depth, 2 * depth, depth, depth, depth, depth + 1)]
    thin = pltpu.VMEM((hidden_blocks, rows, block), jnp.bfloat16)
    held = pltpu.VMEM((depth, rows, shard), jnp.float32)
    full = pltpu.VMEM((devices, rows, shard), tokens.dtype)
    sizes = (2 * depth, depth, depth, depth, depth + 1, 2 * depth, depth, depth + 1)
    result = jax.ShapeDtypeStruct((rows, shard), jnp.bfloat16)
    flops = 2 * rows * shard * devices * hidden_blocks * block * 6
    return pl.pallas_call(
        functools.partial(layer_kernel, depth, hidden_blocks, slots, block),
        out_shape=[result] * 2,
        in_specs=[vmem] * 2 + [smem] + [anywhere] * 3,
        out_specs=[vmem] * 2,
        scratch_shapes=[
            weights,
            weights,
            full,
            full,
            pltpu.VMEM((hidden_blocks, rows, 2 * block), jnp.float32),
            pltpu.VMEM((hidden_blocks // 2, rows, 2 * block), jnp.float32),
            thin,
            thin,
            thin,
            held,
            held,
            dma((4, hidden_blocks)),
        ]
        + gather_sems * 2
        + [pltpu.VMEM((n, rows, shard), jnp.bfloat16) for n in sizes]
        + scatter_sems * 2,
        compiler_params=pltpu.CompilerParams(
            collective_id=0, has_side_effects=True, vmem_limit_bytes=VMEM_LIMIT
        ),
        cost_estimate=pl.CostEstimate(
            flops=flops, bytes_accessed=4 * gate_blocks.size * 2, transcendentals=0
        ),
        name="block_pruned_layer",
    )(tokens, grad_out, at, gate_blocks, up_blocks, down_blocks)


def fits(mesh, tokens, gate_index, gate_blocks):
    tp, dp = mesh.shape["tp"], mesh.shape["dp"]
    rows, shard = tokens.shape[0] // dp, tokens.shape[1] // tp
    hidden_blocks, slots = gate_index.shape[0] // tp, gate_index.shape[1]
    block = gate_blocks.shape[-1]
    held = hidden_blocks * slots * block * block * 2 * 2 + 2 * rows * tokens.shape[1] * 6
    return (
        tp % (CORES * ROWS) == 0
        and tp >= 3 * CORES * ROWS
        and shard % (2 * block) == 0
        and hidden_blocks % 2 == 0
        and rows % 16 == 0
        and held <= VMEM_LIMIT
    )


def densify(blocks, index, count):
    hidden_blocks, slots = index.shape
    block = blocks.shape[-1]
    live = lax.broadcasted_iota(jnp.int32, (hidden_blocks, slots), 1) < count[:, None]
    places = lax.broadcasted_iota(jnp.int32, (hidden_blocks, slots, slots), 2)
    onehot = ((index[:, :, None] == places) & live[:, :, None]).astype(jnp.bfloat16)
    shaped = blocks.reshape(hidden_blocks, slots, block, block)
    return jnp.einsum("hsr,hsab->hrab", onehot, shaped, preferred_element_type=jnp.float32).astype(
        jnp.bfloat16
    )


def column_matrix(dense):
    hidden_blocks, slots, block, _ = dense.shape
    return dense.transpose(1, 2, 0, 3).reshape(slots * block, hidden_blocks * block)


def row_matrix(dense):
    hidden_blocks, slots, block, _ = dense.shape
    return dense.transpose(0, 2, 1, 3).reshape(hidden_blocks * block, slots * block)


def contract_last(left, right):
    return lax.dot_general(
        left, right, (((1,), (1,)), ((), ())), preferred_element_type=jnp.float32
    )


def body(
    tokens,
    grad_out,
    gate_blocks,
    gate_index,
    gate_count,
    up_blocks,
    up_index,
    up_count,
    down_blocks,
    down_index,
    down_count,
):
    hidden_blocks, slots = gate_index.shape
    block = gate_blocks.shape[-1]
    width = hidden_blocks * block
    gate_weight = column_matrix(densify(gate_blocks, gate_index, gate_count))
    up_weight = column_matrix(densify(up_blocks, up_index, up_count))
    down_weight = row_matrix(densify(down_blocks, down_index, down_count))
    all_tokens = lax.all_gather(tokens, "tp", axis=1, tiled=True)
    projected = jnp.concatenate(
        [
            jnp.dot(all_tokens, gate_weight, preferred_element_type=jnp.float32),
            jnp.dot(all_tokens, up_weight, preferred_element_type=jnp.float32),
        ],
        axis=1,
    )
    gate = projected[:, :width]
    upper = projected[:, width:]
    hidden = (gate * jax.nn.sigmoid(gate) * upper).astype(jnp.bfloat16)
    outputs = lax.psum_scatter(
        jnp.dot(hidden, down_weight, preferred_element_type=jnp.float32),
        "tp",
        scatter_dimension=1,
        tiled=True,
    )
    all_grads = lax.all_gather(grad_out, "tp", axis=1, tiled=True)
    grad_hidden = contract_last(all_grads, down_weight)
    gate = projected[:, :width]
    upper = projected[:, width:]
    sigma = jax.nn.sigmoid(gate)
    grad_gate = (grad_hidden * upper * sigma * (1.0 + gate * (1.0 - sigma))).astype(jnp.bfloat16)
    grad_up = (grad_hidden * gate * sigma).astype(jnp.bfloat16)
    grad_gate, grad_up = (grad_gate, grad_up)
    grad_tokens = lax.psum_scatter(
        contract_last(grad_gate, gate_weight) + contract_last(grad_up, up_weight),
        "tp",
        scatter_dimension=1,
        tiled=True,
    )
    return (outputs.astype(jnp.bfloat16), grad_tokens.astype(jnp.bfloat16))


def solution(mesh):
    placed = (
        P("dp", "tp"),
        P("dp", "tp"),
        P("tp", None, None),
        P("tp", None),
        P("tp"),
        P("tp", None, None),
        P("tp", None),
        P("tp"),
        P("tp", None, None),
        P("tp", None),
        P("tp"),
    )

    def run(*args):
        tokens, gate_blocks, gate_index = args[0], args[2], args[3]
        inner = body
        if fits(mesh, tokens, gate_index, gate_blocks):
            inner = functools.partial(fused_body, mesh.shape["tp"] // (CORES * ROWS))
        return jax.shard_map(
            inner, mesh=mesh, in_specs=placed, out_specs=(P("dp", "tp"), P("dp", "tp")), check_vma=False
        )(*args)

    return run
```
